32 devices in a mesh: pipe: 2 (over core), expert: 16 (over z, y, x).
Axes of the slice: x: 2, y: 2, z: 4, core: 2. Of those that a mesh axis runs over, the one named last changes fastest.
Arguments:
- grad_out: bfloat16 [2, 2, 1024, 2048], P('pipe', None, 'expert'), may hold values from -6 to 6
- route_weights: float32 [2, 2, 1024, 8], P('pipe', None, 'expert'), may hold values from 0.1 to 0.6
- expert_ids: int32 [2, 2, 1024, 8], P('pipe', None, 'expert'), may hold values from 0 to 15, all different within a row; in each aligned block of 64 rows (0 to 63, 64 to 127, ..., all dimensions but the last counted through in order) at most 40 rows name the same one
- hot_pos: int32 [2, 4], P('pipe'), may hold values from 0 to 3, as said below
- up_weight: bfloat16 [2, 16, 2048, 768], P('pipe', 'expert'), may hold values from -0.125 to 0.125
- down_weight: bfloat16 [2, 16, 768, 2048], P('pipe', 'expert'), may hold values from -0.21875 to 0.21875
- saved_inputs: bfloat16 [2, 2, 16, 16, 50, 2048], P('pipe', None, 'expert'), may hold values from -6 to 6
- saved_gates: bfloat16 [2, 2, 16, 16, 50, 768], P('pipe', None, 'expert'), may hold values from -8 to 8
Outputs:
- sent_back: bfloat16 [2, 2, 1024, 2048], P('pipe', None, 'expert')
- up_grad: bfloat16 [2, 16, 2048, 768], P('pipe', 'expert')
- down_grad: bfloat16 [2, 16, 768, 2048], P('pipe', 'expert')
- gate_grads: bfloat16 [2, 2, 16, 16, 50, 768], P('pipe', None, 'expert')
- hot_up_grad: bfloat16 [2, 16, 512, 768], P('pipe', 'expert')
- hot_down_grad: bfloat16 [2, 16, 192, 2048], P('pipe', 'expert')
The draws below stay inside these ranges and needn't reach their ends.
Inputs may be any that keep to these rules, and one draw needn't show every extreme that they name: `expert_ids`: each token names 8 different experts. Among the rows of one device in one micro-batch of one section no expert is named more than 40 times, a bound that some block reaches. `hot_pos`: in section 0 the first and the last group copy their expert 4 - 2; in section 1 the first group copies its expert 4 - 1 and the last group its expert 4 - 3.
All inputs are finite; a program needn't handle non-finite values.
Results may differ from the reference program's by a relative error of at most 0.0065.
Values may be sent and summed in bfloat16 or wider, within the bound.
A program may use at most 192 MiB of HBM per device.

```python
import math
import jax
import jax.numpy as jnp
import numpy as np
from jax import lax

D = 2048
FF = 768
TOP = 8
REPL = 4
MB = 2
TOK_DEV = 64
SECTIONS = 2
EXPERTS = 16
HOT = 4
TOKENS = 1024
MOST = 40
SLOTS = 50


def draw_hot_pos(key, part):
    first_key = jax.random.fold_in(key, 101)
    spread = jax.random.randint(first_key, (SECTIONS, HOT), 0, REPL, dtype=jnp.int32)
    section_ix = jnp.arange(SECTIONS, dtype=jnp.int32)[:, None] + jnp.zeros((SECTIONS, HOT), jnp.int32)
    group_ix = jnp.arange(HOT, dtype=jnp.int32)[None, :] + jnp.zeros((SECTIONS, HOT), jnp.int32)
    edge_first = group_ix == 0
    edge_last = group_ix == HOT - 1
    result = jnp.where((section_ix == 0) & (edge_first | edge_last), REPL - 2, spread)
    result = jnp.where((section_ix == 1) & edge_first, REPL - 1, result)
    result = jnp.where((section_ix == 1) & edge_last, REPL - 3, result)
    return result.astype(jnp.int32)


def block_scale(own_key, shape, cuts, smallest, high):
    level, own = 1.0, jax.random.fold_in(own_key, 6)
    for axis_at, blocks in cuts:
        draws = jnp.exp(jax.random.uniform(jax.random.fold_in(own, axis_at), (blocks,), jnp.float32, smallest / len(cuts), high / len(cuts)))
        level = level * jnp.repeat(draws, shape[axis_at] // blocks).reshape([-1 if axis == axis_at else 1 for axis in range(len(shape))])
    return level


def assign_block(stream_key, own, number, rows, count, top, limit, skew):
    ranking = jax.random.permutation(stream_key, count)
    heavy_load, ordinary = portions_of(count, rows * top, limit, skew, True), portions_of(count, rows * top, limit, skew, False)
    places = jnp.arange(count)

    def named(sizes, turn):
        used = int((sizes > 0).sum())
        fixed = max(1, used // 4)
        moved = fixed + (places - fixed + turn * (used - fixed)) % max(1, count - fixed)
        return jnp.zeros((count,), jnp.int32).at[ranking[jnp.where(places < fixed, places, moved)]].set(jnp.asarray(sizes, jnp.int32))

    sizes = jnp.where(number % 4 == 0, named(heavy_load, number // 4), named(ordinary, number - number // 4 - 1))
    mixed = jax.random.permutation(jax.random.fold_in(own, 3), count)
    giver, receiver = mixed[0:count // 2 * 2:2], mixed[1:count // 2 * 2:2]
    slack = jnp.minimum(sizes[giver] - 1, limit - sizes[receiver]) // 2
    slack = jnp.where((giver == ranking[0]) | (receiver == ranking[0]) | (sizes[receiver] == 0), 0, jnp.maximum(slack, 0))
    moved = jax.random.randint(jax.random.fold_in(own, 4), (count // 2,), 0, 1 << 20) % (slack + 1)
    sizes = sizes.at[giver].add(-moved).at[receiver].add(moved)
    items = jnp.searchsorted(jnp.cumsum(sizes), jnp.arange(rows * top), side="right").astype(jnp.int32)
    table = items.reshape(top, rows).T
    table = table[jax.random.permutation(jax.random.fold_in(own, 1), rows)]
    turn = jax.random.randint(jax.random.fold_in(own, 2), (rows, 1), 0, top)
    return jnp.take_along_axis(table, (jnp.arange(top)[None, :] + turn) % top, axis=1)


def portions_of(amount, total, most, lean, full):
    weights = [(1 << 20) // math.isqrt(rank ** lean) + 1 for rank in range(1, amount + 1)]
    largest = most if full else min(most, max(-(-total // amount), total * weights[0] // sum(weights)))
    least = 1 if total - largest >= amount - 1 else 0
    given, spare = [largest] + [least] * (amount - 1), total - largest - least * (amount - 1)
    while spare > 0:
        free = [i for i in range(1, amount) if given[i] < largest] or [i for i in range(1, amount) if given[i] < most]
        mass, budget = sum([weights[i] for i in free]), spare
        for i in free:
            addition = min(most - given[i], max(1, budget * weights[i] // mass), spare)
            given[i] = given[i] + addition
            spare = spare - addition
    return np.array(given)


def scatter_about(key, shape, scale, most, cuts=(), held_as=jnp.bfloat16):
    values = scale * jax.random.normal(key, shape, jnp.float32)
    if cuts:
        values = values * block_scale(key, shape, cuts, -0.22, 0.18)
    return jnp.clip(values, -most, most).astype(held_as)


def setup_inputs(seed: int = 0) -> dict:
    key_list = jax.random.split(jax.random.key(seed), 9)
    grad_out = scatter_about(key_list[0], (SECTIONS, MB, TOKENS, D), 1.0, 6.0, ((0, 2), (2, 16)))
    route_weights = jnp.clip(0.1 + 0.5 * jax.random.uniform(key_list[1], (SECTIONS, MB, TOKENS, TOP), jnp.float32) ** block_scale(key_list[1], (SECTIONS, MB, TOKENS, TOP), ((0, 2), (2, 16)), -0.2, 0.2), 0.1, 0.6)
    expert_ids_keys = jax.random.split(jax.random.fold_in(key_list[2], 1), SECTIONS * MB * TOKENS // TOK_DEV)
    expert_ids_turns = jax.random.permutation(jax.random.fold_in(key_list[2], 3), SECTIONS * MB * TOKENS // TOK_DEV)
    expert_ids = jax.vmap(lambda own, number: assign_block(jax.random.fold_in(key_list[2], 2), own, number, TOK_DEV, EXPERTS, TOP, MOST, 2))(expert_ids_keys, expert_ids_turns).reshape((SECTIONS, MB, TOKENS, TOP))
    hot_pos = draw_hot_pos(jax.random.fold_in(key_list[8], 71), 0)
    up_weight = scatter_about(key_list[4], (SECTIONS, EXPERTS, D, FF), D ** -0.5, 0.125, ((0, 2), (1, 16)))
    down_weight = scatter_about(key_list[5], (SECTIONS, EXPERTS, FF, D), FF ** -0.5, 0.21875, ((0, 2), (1, 16)))
    saved_inputs = scatter_about(key_list[6], (SECTIONS, MB, EXPERTS, EXPERTS, SLOTS, D), 1.0, 6.0, ((0, 2), (2, 16)))
    saved_gates = scatter_about(key_list[7], (SECTIONS, MB, EXPERTS, EXPERTS, SLOTS, FF), 1.5, 8.0, ((0, 2), (2, 16)))
    return dict(grad_out=grad_out, route_weights=route_weights, expert_ids=expert_ids, hot_pos=hot_pos, up_weight=up_weight, down_weight=down_weight, saved_inputs=saved_inputs, saved_gates=saved_gates)


def route_slots(expert_row, sender, hot_table, num_experts, most_rows, slot_count):
    onehot = (expert_row[:, None] == jnp.arange(num_experts, dtype=jnp.int32)[None, :]).astype(jnp.int32)
    order_pos = (jnp.sum(jnp.cumsum(onehot, axis=0).astype(jnp.int32) * onehot, axis=1) - 1).astype(jnp.int32)
    group_id = expert_row // REPL
    hot_count = hot_table.shape[0]
    owner_pos = jnp.sum((group_id[:, None] == jnp.arange(hot_count, dtype=jnp.int32)[None, :]).astype(jnp.int32) * hot_table[None, :], axis=1).astype(jnp.int32)
    is_hot = (expert_row % REPL) == owner_pos
    target = jnp.where(is_hot, REPL * group_id + (sender + order_pos) % REPL, expert_row)
    slot_pos = jnp.where(is_hot, most_rows + order_pos // REPL, order_pos)
    return (target * slot_count + slot_pos).astype(jnp.int32)


def expert_rows(grad_rows, input_rows, gate_rows, up_w, down_w):
    up_value = jnp.dot(input_rows, up_w, preferred_element_type=jnp.float32)
    gate_value = gate_rows.astype(jnp.float32)
    gate_sig = jax.nn.sigmoid(gate_value)
    active = gate_value * gate_sig
    hidden = (active * up_value).astype(jnp.bfloat16)
    grad_hidden = lax.dot_general(grad_rows, down_w, (((1,), (1,)), ((), ())), preferred_element_type=jnp.float32)
    grad_up = (grad_hidden * active).astype(jnp.bfloat16)
    grad_gate = (grad_hidden * up_value * gate_sig * (1.0 + gate_value * (1.0 - gate_sig))).astype(jnp.bfloat16)
    back_rows = lax.dot_general(grad_up, up_w, (((1,), (1,)), ((), ())), preferred_element_type=jnp.float32).astype(jnp.bfloat16)
    down_term = lax.dot_general(hidden, grad_rows, (((0,), (0,)), ((), ())), preferred_element_type=jnp.float32)
    up_term = lax.dot_general(input_rows, grad_up, (((0,), (0,)), ((), ())), preferred_element_type=jnp.float32)
    return back_rows, grad_gate, up_term, down_term


def reference(grad_out, route_weights, expert_ids, hot_pos, up_weight, down_weight, saved_inputs, saved_gates):
    features = grad_out.shape[-1]
    hidden_units = saved_gates.shape[-1]
    target_all = jnp.arange(EXPERTS, dtype=jnp.int32)
    token_all, up_all, down_all, gate_all, hot_up_all, hot_down_all = [], [], [], [], [], []
    for section_idx in range(SECTIONS):
        hot_table = hot_pos[section_idx]
        group_of = (target_all // REPL).astype(jnp.int32)
        hot_expert = (REPL * group_of + hot_table[group_of]).astype(jnp.int32)
        up_section = up_weight[section_idx]
        down_section = down_weight[section_idx]
        index_list, arrive_list = [], []
        for batch_idx in range(MB):
            block_ids = expert_ids[section_idx, batch_idx].reshape(EXPERTS, TOK_DEV * TOP)
            flat_index = jax.vmap(lambda block_row, sender: route_slots(block_row, sender, hot_table, EXPERTS, MOST, SLOTS))(block_ids, target_all)
            scaled = (route_weights[section_idx, batch_idx][:, :, None] * grad_out[section_idx, batch_idx][:, None, :].astype(jnp.float32)).astype(jnp.bfloat16)
            scaled = scaled.reshape(EXPERTS, TOK_DEV * TOP, features)
            buffers = jax.vmap(lambda where_to, values: jnp.zeros((EXPERTS * SLOTS, features), jnp.bfloat16).at[where_to].set(values))(flat_index, scaled)
            buffers = buffers.reshape(EXPERTS, EXPERTS, SLOTS, features).transpose(1, 0, 2, 3)
            index_list.append(flat_index)
            arrive_list.append(buffers)
        received = jnp.stack(arrive_list, 1)
        inputs_section = saved_inputs[section_idx].transpose(1, 0, 2, 3, 4)
        gates_section = saved_gates[section_idx].transpose(1, 0, 2, 3, 4)

        def per_device(packed):
            device, arrived, inputs_dev, gates_dev = packed
            own_up = up_section[device]
            own_down = down_section[device]
            hot_up = up_section[hot_expert[device]]
            hot_down = down_section[hot_expert[device]]
            own_up_sum = jnp.zeros((features, hidden_units), jnp.float32)
            own_down_sum = jnp.zeros((hidden_units, features), jnp.float32)
            rep_up_sum = jnp.zeros((features, hidden_units), jnp.float32)
            rep_down_sum = jnp.zeros((hidden_units, features), jnp.float32)
            back_list, gate_list = [], []
            for batch_idx in range(MB):
                first_part = expert_rows(arrived[batch_idx][:, :MOST].reshape(-1, features), inputs_dev[batch_idx][:, :MOST].reshape(-1, features), gates_dev[batch_idx][:, :MOST].reshape(-1, hidden_units), own_up, own_down)
                second = expert_rows(arrived[batch_idx][:, MOST:].reshape(-1, features), inputs_dev[batch_idx][:, MOST:].reshape(-1, features), gates_dev[batch_idx][:, MOST:].reshape(-1, hidden_units), hot_up, hot_down)
                back_list.append(jnp.concatenate([first_part[0].reshape(EXPERTS, MOST, features), second[0].reshape(EXPERTS, SLOTS - MOST, features)], 1))
                gate_list.append(jnp.concatenate([first_part[1].reshape(EXPERTS, MOST, hidden_units), second[1].reshape(EXPERTS, SLOTS - MOST, hidden_units)], 1))
                own_up_sum = own_up_sum + first_part[2]
                own_down_sum = own_down_sum + first_part[3]
                rep_up_sum = rep_up_sum + second[2]
                rep_down_sum = rep_down_sum + second[3]
            return (jnp.stack(back_list, 0), jnp.stack(gate_list, 0), own_up_sum.astype(jnp.bfloat16), own_down_sum.astype(jnp.bfloat16), rep_up_sum.astype(jnp.bfloat16), rep_down_sum.astype(jnp.bfloat16))

        backs, gate_grads, own_up_all, own_down_all, rep_up_all, rep_down_all = lax.map(per_device, (target_all, received, inputs_section, gates_section))
        group_up = jnp.sum(rep_up_all.reshape(HOT, REPL, features, hidden_units).astype(jnp.float32), axis=1).astype(jnp.bfloat16)
        group_down = jnp.sum(rep_down_all.reshape(HOT, REPL, hidden_units, features).astype(jnp.float32), axis=1).astype(jnp.bfloat16)
        hot_up_all.append(group_up.reshape(EXPERTS, features // REPL, hidden_units))
        hot_down_all.append(group_down.reshape(EXPERTS, hidden_units // REPL, features))
        up_all.append(own_up_all)
        down_all.append(own_down_all)
        gate_all.append(gate_grads.transpose(1, 0, 2, 3, 4))
        batch_grads = []
        for batch_idx in range(MB):
            flat_back = backs[:, batch_idx].transpose(1, 0, 2, 3).reshape(EXPERTS, EXPERTS * SLOTS, features)
            gathered = jnp.take_along_axis(flat_back, index_list[batch_idx][:, :, None], axis=1)
            summed = jnp.sum(gathered.reshape(TOKENS, TOP, features).astype(jnp.float32), axis=1)
            batch_grads.append((summed + grad_out[section_idx, batch_idx].astype(jnp.float32)).astype(jnp.bfloat16))
        token_all.append(jnp.stack(batch_grads, 0))
    sent_back = jnp.roll(jnp.stack(token_all, 0), -1, axis=0)
    return sent_back, jnp.stack(up_all, 0), jnp.stack(down_all, 0), jnp.stack(gate_all, 0), jnp.stack(hot_up_all, 0), jnp.stack(hot_down_all, 0)
```

```python
import jax
import jax.numpy as jnp
from jax import lax
from jax.sharding import PartitionSpec as P

TOP = 8
REPL = 4
MB = 2
BF16 = jnp.bfloat16
F32 = jnp.float32


def partner(value, axis, bit):
    mask = 2**bit
    pairs = [(source, source ^ mask) for source in range(lax.axis_size(axis))]
    return lax.ppermute(value, axis, pairs)


def from_behind(block, axis, distance):
    devices = range(lax.axis_size(axis))
    route = [((i - distance) % len(devices), i) for i in devices]
    return lax.ppermute(block, axis, route)


def pick(array, index, axis):
    return lax.dynamic_index_in_dim(array, index, axis, keepdims=False)


def dot_nn(a, b):
    return jnp.dot(a, b, preferred_element_type=F32)


def dot_nt(a, b):
    return lax.dot_general(a, b, (((1,), (1,)), ((), ())), preferred_element_type=F32)


def dot_tn(a, b):
    return lax.dot_general(a, b, (((0,), (0,)), ((), ())), preferred_element_type=F32)


def gate_parts(gates):
    value = gates.astype(F32)
    sig = jax.nn.sigmoid(value)
    return value * sig, sig * (1.0 + value * (1.0 - sig))


def per_device(
    grad_out, route_weights, expert_ids, hot_pos, up_weight, down_weight, saved_inputs, saved_gates
):
    experts = lax.axis_size("expert")
    device = lax.axis_index("expert")
    features = grad_out.shape[-1]
    hidden_units = saved_gates.shape[-1]
    tokens = grad_out.shape[2]
    slots = saved_inputs.shape[4]
    quarter_rows = slots // (REPL + 1)
    most = REPL * quarter_rows
    quarter = hidden_units // REPL
    groups = [[REPL * g + j for j in range(REPL)] for g in range(experts // REPL)]
    hot_table = hot_pos[0]
    group_id = device // REPL
    local_pos = device % REPL
    low_bit = local_pos % 2
    high_bit = local_pos // 2
    owner_pos = jnp.sum(
        jnp.where(jnp.arange(hot_table.shape[0], dtype=jnp.int32) == group_id, hot_table, 0)
    )
    is_owner = local_pos == owner_pos
    hot_expert = REPL * group_id + owner_pos

    meta = jnp.concatenate([expert_ids[0].astype(F32), route_weights[0]], -1)
    meta = lax.all_gather(meta, "expert", axis=1)
    grads = [lax.all_gather(grad_out[0, b], "expert", axis=0, tiled=True) for b in range(MB)]

    own_up = up_weight[0, 0]
    own_down = down_weight[0, 0]
    owner_mask = is_owner.astype(BF16)
    up_t = (own_up.T * owner_mask).reshape(2, 2, quarter, features)
    down = (own_down * owner_mask).reshape(2, 2, quarter, features)
    up_in = partner(pick(up_t, 1 - low_bit, 1), "expert", 0)
    down_in = partner(pick(down, 1 - high_bit, 0), "expert", 1)
    up_half = pick(up_t, low_bit, 1) + up_in
    down_half = pick(down, high_bit, 0) + down_in
    up_in = partner(pick(up_half, 1 - high_bit, 0), "expert", 1)
    down_in = partner(pick(down_half, 1 - low_bit, 0), "expert", 0)
    hot_up = pick(up_half, high_bit, 0) + up_in
    hot_down = pick(down_half, low_bit, 0) + down_in

    inputs = saved_inputs[0, :, 0]
    gates = saved_gates[0, :, 0]
    hot_rows = experts * quarter_rows
    hot_inputs = inputs[:, :, most:].reshape(MB * hot_rows, features)
    hot_inputs = lax.all_gather(hot_inputs, "expert", axis=0, axis_index_groups=groups)
    hot_inputs = hot_inputs.reshape(REPL, MB, hot_rows, features)
    hot_gates = gates[:, :, most:].reshape(MB * hot_rows, REPL, quarter).transpose(1, 0, 2)
    hot_gates = lax.all_to_all(hot_gates, "expert", 0, 0, axis_index_groups=groups, tiled=True)
    hot_gates = hot_gates.reshape(REPL, MB, hot_rows, quarter)

    ids = meta[..., :TOP]
    weights = meta[..., TOP:]
    own_hit = (ids == device.astype(F32)) & jnp.logical_not(is_owner)
    hot_hit = ids == hot_expert.astype(F32)
    own_weight = jnp.sum(jnp.where(own_hit, weights, 0.0), -1)
    hot_weight = jnp.sum(jnp.where(hot_hit, weights, 0.0), -1)
    own_named = jnp.any(own_hit, -1)
    hot_named = jnp.any(hot_hit, -1)
    own_place = jnp.where(own_named, jnp.cumsum(own_named.astype(jnp.int32), -1) - 1, -1)
    hot_place = jnp.where(hot_named, jnp.cumsum(hot_named.astype(jnp.int32), -1) - 1, -1)
    own_select = (own_place[..., None] == jnp.arange(slots, dtype=jnp.int32)).astype(BF16)
    block = jnp.arange(experts, dtype=jnp.int32)
    replica = jnp.arange(REPL, dtype=jnp.int32)
    order = (
        REPL * jnp.arange(quarter_rows, dtype=jnp.int32)[None, None, :]
        + (replica[:, None, None] - block[None, :, None]) % REPL
    )
    same = block[:, None, None, None, None] == block[None, None, None, :, None]
    hot_select = [
        ((hot_place[b][:, :, None, None, None] == order[None, None]) & same)
        .astype(BF16)
        .reshape(experts * tokens, REPL * hot_rows)
        for b in range(MB)
    ]

    parts = []
    returned = []
    gate_grads = []
    hot_gate_grads = []
    for b in range(MB):
        own_x = jnp.einsum(
            "etc,ecd->etd", own_select[b], inputs[b], preferred_element_type=F32
        ).astype(BF16).reshape(experts * tokens, features)
        own_a = jnp.einsum(
            "etc,ecd->etd", own_select[b], gates[b], preferred_element_type=F32
        ).astype(BF16).reshape(experts * tokens, hidden_units)
        hot_x = dot_nn(
            hot_select[b], hot_inputs[:, b].reshape(REPL * hot_rows, features)
        ).astype(BF16)
        hot_a = dot_nn(
            hot_select[b], hot_gates[:, b].reshape(REPL * hot_rows, quarter)
        ).astype(BF16)
        grad = grads[b].astype(F32)
        own_g = (own_weight[b].reshape(-1, 1) * grad).astype(BF16)
        hot_g = (hot_weight[b].reshape(-1, 1) * grad).astype(BF16)
        own_act, own_slope = gate_parts(own_a)
        hot_act, hot_slope = gate_parts(hot_a)
        own_uv = dot_nn(own_x, own_up)
        hot_uv = dot_nt(hot_x, hot_up)
        own_gh = dot_nt(own_g, own_down)
        hot_gh = dot_nt(hot_g, hot_down)
        own_gu = (own_gh * own_act).astype(BF16)
        hot_gu = (hot_gh * hot_act).astype(BF16)
        own_hidden = (own_act * own_uv).astype(BF16)
        hot_hidden = (hot_act * hot_uv).astype(BF16)
        own_gg = (own_gh * own_uv * own_slope).astype(BF16)
        hot_gg = (hot_gh * hot_uv * hot_slope).astype(BF16)
        term = (dot_nt(own_gu, own_up) + dot_nn(hot_gu, hot_up)).astype(BF16)
        returned.append(
            lax.psum_scatter(term.reshape(experts, tokens, features), "expert")
        )
        gate_grads.append(
            jnp.einsum(
                "etc,etf->ecf",
                own_select[b],
                own_gg.reshape(experts, tokens, hidden_units),
                preferred_element_type=F32,
            ).astype(BF16)
        )
        hot_gate_grads.append(
            dot_tn(hot_select[b], hot_gg).astype(BF16).reshape(REPL, hot_rows, quarter)
        )
        parts.append((own_x, own_gu, own_hidden, own_g, hot_x, hot_gu, hot_hidden, hot_g))
    own_x, own_gu, own_hidden, own_g, hot_x, hot_gu, hot_hidden, hot_g = (
        [member[n] for member in parts] for n in range(8)
    )
    hot_up_grad = sum(dot_tn(hot_gu[b], hot_x[b]) for b in range(MB)).astype(BF16)
    hot_down_grad = sum(dot_tn(hot_hidden[b], hot_g[b]) for b in range(MB)).astype(BF16)
    up_grad = sum(dot_tn(own_x[b], own_gu[b]) for b in range(MB)).astype(BF16)
    down_grad = sum(dot_tn(own_hidden[b], own_g[b]) for b in range(MB)).astype(BF16)

    hot_up_grad = lax.all_to_all(
        hot_up_grad, "expert", 1, 0, axis_index_groups=groups, tiled=True
    ).T
    back = jnp.stack(hot_gate_grads, 1).reshape(REPL, MB * hot_rows, quarter)
    back = lax.all_to_all(back, "expert", 0, 0, axis_index_groups=groups, tiled=True)
    back = back.transpose(1, 0, 2).reshape(MB, experts, quarter_rows, hidden_units)
    gate_grad = jnp.concatenate([jnp.stack(gate_grads, 0)[:, :, :most], back], 2)

    token_grads = jnp.stack(
        [
            (returned[b].astype(F32) + grad_out[0, b].astype(F32)).astype(BF16)
            for b in range(MB)
        ],
        0,
    )
    sent_back = from_behind(token_grads, "pipe", -1)
    return (
        sent_back[None],
        up_grad[None, None],
        down_grad[None, None],
        gate_grad[None, :, None],
        hot_up_grad[None, None],
        hot_down_grad[None, None],
    )


def solution(mesh):
    return jax.shard_map(
        per_device,
        mesh=mesh,
        in_specs=(
            P("pipe", None, "expert", None),
            P("pipe", None, "expert", None),
            P("pipe", None, "expert", None),
            P("pipe", None),
            P("pipe", "expert", None, None),
            P("pipe", "expert", None, None),
            P("pipe", None, "expert", None, None, None),
            P("pipe", None, "expert", None, None, None),
        ),
        out_specs=(
            P("pipe", None, "expert", None),
            P("pipe", "expert", None, None),
            P("pipe", "expert", None, None),
            P("pipe", None, "expert", None, None, None),
            P("pipe", "expert", None, None),
            P("pipe", "expert", None, None),
        ),
        check_vma=False,
    )
```

```python
import jax
import jax.numpy as jnp
from jax import lax
from jax.sharding import PartitionSpec as P

TOP = 8
REPL = 4
MB = 2
BF16 = jnp.bfloat16
F32 = jnp.float32


def partner(value, axis, bit):
    mask = 2**bit
    pairs = [(source, source ^ mask) for source in range(lax.axis_size(axis))]
    return lax.ppermute(value, axis, pairs)


def from_behind(block, axis, distance):
    devices = range(lax.axis_size(axis))
    route = [((i - distance) % len(devices), i) for i in devices]
    return lax.ppermute(block, axis, route)


def pick(array, index, axis):
    return lax.dynamic_index_in_dim(array, index, axis, keepdims=False)


def offsets(bits):
    found = [0]
    for bit in bits:
        found = found + [value ^ 2**bit for value in found]
    return found


def spread(block, bits):
    for bit in bits:
        block = jnp.concatenate([block, partner(block, "expert", bit)], 0)
    return block


def collect(total, bits):
    for bit in reversed(bits):
        half = total.shape[0] // 2
        kept, sent = total[:half], total[half:].astype(BF16)
        total = kept.astype(F32) + partner(sent, "expert", bit).astype(F32)
        if half > 1:
            total = total.astype(BF16)
    return total


def dot_nn(a, b):
    return jnp.dot(a, b, preferred_element_type=F32)


def dot_nt(a, b):
    return lax.dot_general(a, b, (((1,), (1,)), ((), ())), preferred_element_type=F32)


def dot_tn(a, b):
    return lax.dot_general(a, b, (((0,), (0,)), ((), ())), preferred_element_type=F32)


def gate_parts(gates):
    value = gates.astype(F32)
    sig = jax.nn.sigmoid(value)
    return value * sig, sig * (1.0 + value * (1.0 - sig))


def per_device(
    grad_out, route_weights, expert_ids, hot_pos, up_weight, down_weight, saved_inputs, saved_gates
):
    experts = lax.axis_size("expert")
    device = lax.axis_index("expert")
    features = grad_out.shape[-1]
    hidden_units = saved_gates.shape[-1]
    tokens = grad_out.shape[2]
    slots = saved_inputs.shape[4]
    quarter_rows = slots // (REPL + 1)
    most = REPL * quarter_rows
    quarter = hidden_units // REPL
    groups = [[REPL * g + j for j in range(REPL)] for g in range(experts // REPL)]
    hot_table = hot_pos[0]
    group_id = device // REPL
    local_pos = device % REPL
    low_bit = local_pos % 2
    high_bit = local_pos // 2
    owner_pos = jnp.sum(
        jnp.where(jnp.arange(hot_table.shape[0], dtype=jnp.int32) == group_id, hot_table, 0)
    )
    is_owner = local_pos == owner_pos
    hot_expert = REPL * group_id + owner_pos

    bits = experts.bit_length() - 1
    orders = [list(range(2, bits)) + pair for pair in ([1, 0], [0, 1])]
    group_orders = [[0, 1], [1, 0]]
    meta = jnp.concatenate([expert_ids[0].astype(F32), route_weights[0]], -1)
    meta = spread(meta.transpose(0, 2, 1)[None], orders[0])
    grads = [spread(grad_out[0, b][None], orders[b % 2]) for b in range(MB)]

    own_up = up_weight[0, 0]
    own_down = down_weight[0, 0]
    owner_mask = is_owner.astype(BF16)
    up_t = (own_up.T * owner_mask).reshape(2, 2, quarter, features)
    down = (own_down * owner_mask).reshape(2, 2, quarter, features)
    up_in = partner(pick(up_t, 1 - low_bit, 1), "expert", 0)
    down_in = partner(pick(down, 1 - high_bit, 0), "expert", 1)
    up_half = pick(up_t, low_bit, 1) + up_in
    down_half = pick(down, high_bit, 0) + down_in
    up_in = partner(pick(up_half, 1 - high_bit, 0), "expert", 1)
    down_in = partner(pick(down_half, 1 - low_bit, 0), "expert", 0)
    hot_up = pick(up_half, high_bit, 0) + up_in
    hot_down = pick(down_half, low_bit, 0) + down_in

    inputs = saved_inputs[0, :, 0]
    gates = saved_gates[0, :, 0]
    hot_rows = experts * quarter_rows
    hot_inputs = inputs[:, :, most:].reshape(MB, hot_rows, features)
    hot_inputs = [
        spread(hot_inputs[b][None], group_orders[b % 2]).reshape(REPL * hot_rows, features)
        for b in range(MB)
    ]
    hot_gates = gates[:, :, most:].reshape(MB * hot_rows, REPL, quarter).transpose(1, 0, 2)
    hot_gates = lax.all_to_all(hot_gates, "expert", 0, 0, axis_index_groups=groups, tiled=True)
    hot_gates = hot_gates.reshape(REPL, MB, hot_rows, quarter)

    own_select, hot_select, hot_gate_select, own_weight, hot_weight = [], [], [], [], []
    earlier = jnp.triu(jnp.ones((tokens, tokens), BF16), 1)
    for b in range(MB):
        order = offsets(orders[b % 2])
        first = offsets(orders[0])
        table = meta[:, b]
        if order != first:
            table = jnp.stack([table[first.index(value)] for value in order], 0)
        table = table.transpose(1, 0, 2)
        block = (jnp.array(order, jnp.int32) ^ device)[:, None]
        own_hit = (table[:TOP] == device.astype(F32)) & jnp.logical_not(is_owner)
        hot_hit = table[:TOP] == hot_expert.astype(F32)
        own_weight.append(jnp.sum(jnp.where(own_hit, table[TOP:], 0.0), 0).reshape(-1, 1))
        hot_weight.append(jnp.sum(jnp.where(hot_hit, table[TOP:], 0.0), 0).reshape(-1, 1))
        own_named = jnp.sum(own_hit.astype(F32), 0)
        hot_named = jnp.sum(hot_hit.astype(F32), 0)
        own_rank = dot_nn(own_named.astype(BF16), earlier).astype(jnp.int32)
        hot_rank = dot_nn(hot_named.astype(BF16), earlier).astype(jnp.int32)
        own_slot = jnp.where(own_named > 0, block * slots + own_rank, -1)
        target = (block + hot_rank) % REPL
        row = block * quarter_rows + hot_rank // REPL
        away = target ^ local_pos
        if group_orders[b % 2] == [1, 0]:
            away = away // 2 + 2 * (away % 2)
        near_slot = jnp.where(hot_named > 0, away * hot_rows + row, -1)
        far_slot = jnp.where(hot_named > 0, target * hot_rows + row, -1)
        slot_range = jnp.arange(experts * slots, dtype=jnp.int32)[None]
        hot_range = jnp.arange(REPL * hot_rows, dtype=jnp.int32)[None]
        own_select.append((own_slot.reshape(-1, 1) == slot_range).astype(BF16))
        hot_select.append((near_slot.reshape(-1, 1) == hot_range).astype(BF16))
        hot_gate_select.append((far_slot.reshape(-1, 1) == hot_range).astype(BF16))

    flat_inputs = inputs.reshape(MB, experts * slots, features)
    flat_gates = gates.reshape(MB, experts * slots, hidden_units)
    parts = []
    returned = []
    gate_grads = []
    hot_gate_grads = []
    for b in range(MB):
        own_x = dot_nn(own_select[b], flat_inputs[b]).astype(BF16)
        own_a = dot_nn(own_select[b], flat_gates[b]).astype(BF16)
        hot_x = dot_nn(hot_select[b], hot_inputs[b]).astype(BF16)
        hot_a = dot_nn(
            hot_gate_select[b], hot_gates[:, b].reshape(REPL * hot_rows, quarter)
        ).astype(BF16)
        grad = grads[b].reshape(experts * tokens, features).astype(F32)
        own_g = (own_weight[b] * grad).astype(BF16)
        hot_g = (hot_weight[b] * grad).astype(BF16)
        own_act, own_slope = gate_parts(own_a)
        hot_act, hot_slope = gate_parts(hot_a)
        own_uv = dot_nn(own_x, own_up)
        hot_uv = dot_nt(hot_x, hot_up)
        own_gh = dot_nt(own_g, own_down)
        hot_gh = dot_nt(hot_g, hot_down)
        own_gu = (own_gh * own_act).astype(BF16)
        hot_gu = (hot_gh * hot_act).astype(BF16)
        own_hidden = (own_act * own_uv).astype(BF16)
        hot_hidden = (hot_act * hot_uv).astype(BF16)
        own_gg = (own_gh * own_uv * own_slope).astype(BF16)
        hot_gg = (hot_gh * hot_uv * hot_slope).astype(BF16)
        term = (dot_nt(own_gu, own_up) + dot_nn(hot_gu, hot_up)).astype(BF16)
        returned.append(
            collect(term.reshape(experts, tokens, features), orders[b % 2])[0]
        )
        gate_grads.append(
            dot_tn(own_select[b], own_gg).astype(BF16).reshape(experts, slots, hidden_units)
        )
        hot_gate_grads.append(
            dot_tn(hot_gate_select[b], hot_gg).astype(BF16).reshape(REPL, hot_rows, quarter)
        )
        parts.append((own_x, own_gu, own_hidden, own_g, hot_x, hot_gu, hot_hidden, hot_g))
    own_x, own_gu, own_hidden, own_g, hot_x, hot_gu, hot_hidden, hot_g = (
        [member[n] for member in parts] for n in range(8)
    )
    hot_up_grad = sum(dot_tn(hot_gu[b], hot_x[b]) for b in range(MB)).astype(BF16)
    hot_down_grad = sum(dot_tn(hot_hidden[b], hot_g[b]) for b in range(MB)).astype(BF16)
    up_grad = sum(dot_tn(own_x[b], own_gu[b]) for b in range(MB)).astype(BF16)
    down_grad = sum(dot_tn(own_hidden[b], own_g[b]) for b in range(MB)).astype(BF16)

    hot_up_grad = lax.all_to_all(
        hot_up_grad, "expert", 1, 0, axis_index_groups=groups, tiled=True
    ).T
    back = jnp.stack(hot_gate_grads, 1).reshape(REPL, MB * hot_rows, quarter)
    back = lax.all_to_all(back, "expert", 0, 0, axis_index_groups=groups, tiled=True)
    back = back.transpose(1, 0, 2).reshape(MB, experts, quarter_rows, hidden_units)
    gate_grad = jnp.concatenate([jnp.stack(gate_grads, 0)[:, :, :most], back], 2)

    sent_back = jnp.stack(
        [
            from_behind(
                (returned[b] + grad_out[0, b].astype(F32)).astype(BF16), "pipe", -1
            )
            for b in range(MB)
        ],
        0,
    )
    return (
        sent_back[None],
        up_grad[None, None],
        down_grad[None, None],
        gate_grad[None, :, None],
        hot_up_grad[None, None],
        hot_down_grad[None, None],
    )


def solution(mesh):
    return jax.shard_map(
        per_device,
        mesh=mesh,
        in_specs=(
            P("pipe", None, "expert", None),
            P("pipe", None, "expert", None),
            P("pipe", None, "expert", None),
            P("pipe", None),
            P("pipe", "expert", None, None),
            P("pipe", "expert", None, None),
            P("pipe", None, "expert", None, None, None),
            P("pipe", None, "expert", None, None, None),
        ),
        out_specs=(
            P("pipe", None, "expert", None),
            P("pipe", "expert", None, None),
            P("pipe", "expert", None, None),
            P("pipe", None, "expert", None, None, None),
            P("pipe", "expert", None, None),
            P("pipe", "expert", None, None),
        ),
        check_vma=False,
    )
```
